1024 devices in a mesh: pipe: 16 (over x, y_lo, core), expert: 64 (over z, y_hi).
Axes of the slice: x: 4, y: 4 (y_hi: 2, y_lo: 2; y = y_hi * 2 + y_lo), z: 32, core: 2. Of those that a mesh axis runs over, the one named last changes fastest.
Arguments:
- fwd_tokens: bfloat16 [16, 512, 7168], P('pipe', 'expert'), may hold values from -6 to 6
- fwd_routes: int32 [16, 512, 1], P('pipe', 'expert'), may hold values from 0 to 3, as said below
- fwd_weight: float32 [16, 512, 1], P('pipe', 'expert'), may hold values from 0.2 to 1
- bwd_grad: bfloat16 [16, 512, 7168], P('pipe', 'expert'), may hold values from -6 to 6
- bwd_routes: int32 [16, 512, 1], P('pipe', 'expert'), may hold values from 0 to 3, as said below
- bwd_weight: float32 [16, 512, 1], P('pipe', 'expert'), may hold values from 0.2 to 1
- gate_saved: float32 [16, 256, 4096], P('pipe', None, 'expert'), may hold values from -6 to 6
- up_saved: float32 [16, 256, 4096], P('pipe', None, 'expert'), may hold values from -6 to 6
- gate_proj: bfloat16 [16, 64, 3584, 128], P('pipe', 'expert'), may hold values from -0.0625 to 0.0625
- up_proj: bfloat16 [16, 64, 3584, 128], P('pipe', 'expert'), may hold values from -0.0625 to 0.0625
- down_proj: bfloat16 [16, 64, 128, 3584], P('pipe', 'expert'), may hold values from -0.1875 to 0.1875
Outputs:
- fwd_next: bfloat16 [16, 512, 7168], P('pipe', 'expert')
- bwd_next: bfloat16 [16, 512, 7168], P('pipe', 'expert')
The draws below stay inside these ranges and needn't reach their ends.
Inputs may be any that keep to these rules, and one draw needn't show every extreme that they name: `fwd_routes`: each token names one expert of the window. Among the 8 tokens of one device no expert is named by more than 4 routes, and in each section one expert is named by exactly 4 routes of every device. `bwd_routes`: as fwd_routes.
All inputs are finite; a program needn't handle non-finite values.
Results may differ from the reference program's by a relative error of at most 0.013.
Values may be sent and summed in bfloat16 or wider, within the bound.
A program may use at most 64 MiB of HBM per device.

```python
import math
import jax
import jax.numpy as jnp
from jax import lax

D = 7168
FF_WIN = 1024
ROUTES = 1
TOK_DEV = 8
SECTIONS = 16
HSH = 8
SPLITS = 2
EXP_WIN = 4
FF_SHARD = 128
CAP = 4
SLOTS = 256
TOKENS = 512
N_EXPERT = 64


def route_table(key):
    hot_key, order_key, token_key, offset_key = jax.random.split(key, 4)
    per_section = TOKENS // TOK_DEV
    blocks = SECTIONS * per_section
    others = max(EXP_WIN - 1, 1)
    positions = TOK_DEV * ROUTES
    hottest = jax.random.randint(hot_key, (SECTIONS,), 0, EXP_WIN).astype(jnp.int32)
    hottest = jnp.repeat(hottest, per_section)[:, None]
    order_scores = jax.random.randint(order_key, (blocks, others), 0, 1 << 20) * others + jnp.arange(others, dtype=jnp.int32)[None, :]
    order = jnp.argsort(order_scores, axis=1).astype(jnp.int32)
    token_scores = jax.random.randint(token_key, (blocks, TOK_DEV), 0, 1 << 20) * TOK_DEV + jnp.arange(TOK_DEV, dtype=jnp.int32)[None, :]
    token_order = jnp.argsort(token_scores, axis=1).astype(jnp.int32)
    offset = jax.random.randint(offset_key, (blocks, 1), 0, CAP).astype(jnp.int32)
    position = jnp.arange(positions, dtype=jnp.int32)[None, :]
    rank_used = jnp.where(position < CAP, 0, 1 + (position - CAP + offset) // CAP)
    rank_other = jnp.clip(rank_used - 1, 0, others - 1)
    picked = jnp.take_along_axis(order, jnp.broadcast_to(rank_other, (blocks, positions)), axis=1)
    expert = jnp.where(rank_used == 0, hottest, (hottest + 1 + picked) % EXP_WIN)
    expert = jnp.transpose(expert.reshape(blocks, ROUTES, TOK_DEV), (0, 2, 1))
    index = jnp.broadcast_to(token_order[:, :, None], (blocks, TOK_DEV, ROUTES))
    expert = jnp.take_along_axis(expert, index, axis=1)
    return expert.reshape(SECTIONS, TOKENS, ROUTES).astype(jnp.int32)


def draw_fwd_routes(key, part):
    key = jax.random.fold_in(key, 11)
    return route_table(key)


def draw_bwd_routes(key, part):
    key = jax.random.fold_in(key, 23)
    return route_table(key)


def shard_levels(key, extent, cuts, least, top_value):
    def one(dim, blocks):
        steps = jax.random.uniform(jax.random.fold_in(jax.random.fold_in(key, 6), dim), (blocks,), jnp.float32, least / len(cuts), top_value / len(cuts))
        return jnp.repeat(jnp.exp(steps), extent[dim] // blocks).reshape((-1,) + (1,) * (len(extent) - dim - 1))

    factor_of = one(*cuts[0])
    for cut in cuts[1:]:
        factor_of = factor_of * one(*cut)
    return factor_of


def centred(own_key, shape, deviation, bound, shards=(), kind=jnp.bfloat16):
    drawn = jax.random.normal(own_key, shape, jnp.float32) * deviation
    if len(shards) > 0:
        drawn = shard_levels(own_key, shape, shards, -0.22, 0.18) * drawn
    return jnp.clip(drawn, min=-bound, max=bound).astype(kind)


def setup_inputs(seed: int = 0) -> dict:
    key_list = jax.random.split(jax.random.key(seed), 12)
    fwd_tokens = centred(key_list[0], (SECTIONS, TOKENS, D), 1.0, 6.0, ((0, 16), (1, 64)))
    fwd_routes = draw_fwd_routes(jax.random.fold_in(key_list[11], 71), 0)
    fwd_weight = jnp.clip(jnp.exp(math.log(1.0) - 1.609438 * jax.random.uniform(key_list[2], (SECTIONS, TOKENS, ROUTES), jnp.float32) ** shard_levels(key_list[2], (SECTIONS, TOKENS, ROUTES), ((0, 16), (1, 64)), -0.2, 0.2)), 0.2, 1.0)
    bwd_grad = centred(key_list[3], (SECTIONS, TOKENS, D), 1.0, 6.0, ((0, 16), (1, 64)))
    bwd_routes = draw_bwd_routes(jax.random.fold_in(key_list[11], 71), 0)
    bwd_weight = jnp.clip(jnp.exp(math.log(1.0) - 1.609438 * jax.random.uniform(key_list[5], (SECTIONS, TOKENS, ROUTES), jnp.float32) ** shard_levels(key_list[5], (SECTIONS, TOKENS, ROUTES), ((0, 16), (1, 64)), -0.2, 0.2)), 0.2, 1.0)
    gate_saved = centred(key_list[6], (SECTIONS, SLOTS, EXP_WIN * FF_WIN), 1.0, 6.0, ((0, 16), (2, 64)), jnp.float32)
    up_saved = centred(key_list[7], (SECTIONS, SLOTS, EXP_WIN * FF_WIN), 1.0, 6.0, ((0, 16), (2, 64)), jnp.float32)
    gate_proj = centred(key_list[8], (SECTIONS, N_EXPERT, D // SPLITS, FF_SHARD), D ** -0.5, 0.0625, ((0, 16), (1, 64)))
    up_proj = centred(key_list[9], (SECTIONS, N_EXPERT, D // SPLITS, FF_SHARD), D ** -0.5, 0.0625, ((0, 16), (1, 64)))
    down_proj = centred(key_list[10], (SECTIONS, N_EXPERT, FF_SHARD, D // SPLITS), FF_WIN ** -0.5, 0.1875, ((0, 16), (1, 64)))
    return {"fwd_tokens": fwd_tokens, "fwd_routes": fwd_routes, "fwd_weight": fwd_weight, "bwd_grad": bwd_grad, "bwd_routes": bwd_routes, "bwd_weight": bwd_weight, "gate_saved": gate_saved, "up_saved": up_saved, "gate_proj": gate_proj, "up_proj": up_proj, "down_proj": down_proj}


def build_sel(routes_dev, experts, capacity):
    flat = routes_dev.reshape(-1).astype(jnp.int32)
    onehot = (flat[:, None] == jnp.arange(experts, dtype=jnp.int32)[None, :]).astype(jnp.int32)
    before = jnp.cumsum(onehot, axis=0) - onehot
    position = jnp.sum(before * onehot, axis=1).astype(jnp.int32)
    place = flat * capacity + position
    return (jnp.arange(experts * capacity, dtype=jnp.int32)[:, None] == place[None, :]).astype(jnp.bfloat16)


def assemble(gate_section, up_section, down_section):
    def rows_form(matrix):
        matrix = matrix.reshape(EXP_WIN, HSH, SPLITS, D // SPLITS, FF_SHARD)
        return jnp.transpose(matrix, (0, 2, 3, 1, 4)).reshape(EXP_WIN, D, FF_WIN)

    down = down_section.reshape(EXP_WIN, HSH, SPLITS, FF_SHARD, D // SPLITS)
    down = jnp.transpose(down, (0, 1, 3, 2, 4)).reshape(EXP_WIN, HSH, FF_SHARD, D)
    return rows_form(gate_section), rows_form(up_section), down


def expert_forward(rows, w_gate, w_up, w_down):
    gate = jnp.dot(rows, w_gate, preferred_element_type=jnp.float32)
    upper = jnp.dot(rows, w_up, preferred_element_type=jnp.float32)
    hidden = (jax.nn.silu(gate) * upper).astype(jnp.bfloat16).reshape(SLOTS, HSH, FF_SHARD)
    partial_out = jnp.einsum("shk,hkd->hsd", hidden.astype(jnp.float32), w_down.astype(jnp.float32)).astype(jnp.bfloat16)
    return jnp.sum(partial_out.astype(jnp.float32), axis=0).astype(jnp.bfloat16)


def expert_backward(rows, w_gate, w_up, w_down, gate_pre, up_pre):
    flat_down = w_down.reshape(FF_WIN, D)
    hidden_grad = jnp.dot(rows, flat_down.T, preferred_element_type=jnp.float32)
    logistic = jax.nn.sigmoid(gate_pre)
    gate_grad = (hidden_grad * up_pre * logistic * (1.0 + gate_pre * (1.0 - logistic))).astype(jnp.bfloat16)
    up_grad = (hidden_grad * gate_pre * logistic).astype(jnp.bfloat16)
    gate_grad = gate_grad.reshape(SLOTS, HSH, FF_SHARD).astype(jnp.float32)
    up_grad = up_grad.reshape(SLOTS, HSH, FF_SHARD).astype(jnp.float32)
    gate_blocks = w_gate.reshape(D, HSH, FF_SHARD).astype(jnp.float32)
    up_blocks = w_up.reshape(D, HSH, FF_SHARD).astype(jnp.float32)
    partial_in = jnp.einsum("shk,dhk->hsd", gate_grad, gate_blocks) + jnp.einsum("shk,dhk->hsd", up_grad, up_blocks)
    partial_in = partial_in.astype(jnp.bfloat16)
    return jnp.sum(partial_in.astype(jnp.float32), axis=0).astype(jnp.bfloat16)


def to_experts(per_source):
    return jnp.transpose(per_source.reshape(N_EXPERT, EXP_WIN, CAP, D), (1, 0, 2, 3)).reshape(EXP_WIN, SLOTS, D)


def to_sources(per_expert):
    return jnp.transpose(per_expert.reshape(EXP_WIN, N_EXPERT, CAP, D), (1, 0, 2, 3)).reshape(N_EXPERT, EXP_WIN * CAP, D)


def place_rows(select, rows):
    return jax.vmap(lambda left, right: jnp.dot(left, right, preferred_element_type=jnp.float32))(select, rows).astype(jnp.bfloat16)


def pick_rows(select, values):
    return jax.vmap(lambda left, right: lax.dot_general(left, right, (((0,), (0,)), ((), ())), preferred_element_type=jnp.float32))(select, values)


def one_section(inputs):
    tokens, routes_f, weight_f, grads, routes_b, weight_b, gate_keep, up_keep, gate_section, up_section, down_section = inputs
    w_gate, w_up, w_down = assemble(gate_section, up_section, down_section)
    tokens = tokens.reshape(N_EXPERT, TOK_DEV, D)
    select_f = jax.vmap(lambda rows: build_sel(rows, EXP_WIN, CAP))(routes_f.reshape(N_EXPERT, TOK_DEV, ROUTES))
    slots_f = place_rows(select_f, jnp.repeat(tokens, ROUTES, axis=1))
    out_f = lax.map(lambda item: expert_forward(*item), (to_experts(slots_f), w_gate, w_up, w_down))
    routed = pick_rows(select_f, to_sources(out_f)).reshape(N_EXPERT, TOK_DEV, ROUTES, D)
    mixed = tokens.astype(jnp.float32) + jnp.sum(weight_f.reshape(N_EXPERT, TOK_DEV, ROUTES, 1) * routed, axis=2)
    grads = grads.reshape(N_EXPERT, TOK_DEV, D)
    select_b = jax.vmap(lambda rows: build_sel(rows, EXP_WIN, CAP))(routes_b.reshape(N_EXPERT, TOK_DEV, ROUTES))
    scaled = (weight_b.reshape(N_EXPERT, TOK_DEV * ROUTES, 1) * jnp.repeat(grads, ROUTES, axis=1).astype(jnp.float32)).astype(jnp.bfloat16)
    slots_b = place_rows(select_b, scaled)
    gate_pre = jnp.transpose(gate_keep.reshape(SLOTS, EXP_WIN, FF_WIN), (1, 0, 2))
    up_pre = jnp.transpose(up_keep.reshape(SLOTS, EXP_WIN, FF_WIN), (1, 0, 2))
    out_b = lax.map(lambda item: expert_backward(*item), (to_experts(slots_b), w_gate, w_up, w_down, gate_pre, up_pre))
    routed_b = pick_rows(select_b, to_sources(out_b)).reshape(N_EXPERT, TOK_DEV, ROUTES, D)
    grad_in = grads.astype(jnp.float32) + jnp.sum(routed_b, axis=2)
    return mixed.astype(jnp.bfloat16).reshape(TOKENS, D), grad_in.astype(jnp.bfloat16).reshape(TOKENS, D)


def reference(fwd_tokens, fwd_routes, fwd_weight, bwd_grad, bwd_routes, bwd_weight, gate_saved, up_saved, gate_proj, up_proj, down_proj):
    mixed_all, grad_all = lax.map(one_section, (fwd_tokens, fwd_routes, fwd_weight, bwd_grad, bwd_routes, bwd_weight, gate_saved, up_saved, gate_proj, up_proj, down_proj))
    return jnp.roll(mixed_all, 1, axis=0), jnp.roll(grad_all, 1, axis=0)
```

```python
import jax
import jax.numpy as jnp
from jax import lax
from jax.sharding import PartitionSpec as P


def pair_swap(value):
    count = lax.axis_size("expert")
    return lax.ppermute(value, "expert", [(s, s ^ 1) for s in range(count)])


def from_behind(value, axis, steps):
    count = lax.axis_size(axis)
    return lax.ppermute(value, axis, [(s, (s + steps) % count) for s in range(count)])


def columns():
    count = lax.axis_size("expert")
    return [list(range(0, count, 2)), list(range(1, count, 2))]


def halves(rows, own_i):
    half = rows.shape[1] // 2
    first, second = rows[:, :half], rows[:, half:]
    keep = jnp.where(own_i == 0, first, second)
    send = jnp.where(own_i == 0, second, first)
    got = pair_swap(send)
    return jnp.where(own_i == 0, jnp.concatenate([keep, got]), jnp.concatenate([got, keep]))


def rejoin(rows, own_i):
    tok = rows.shape[0] // 2
    keep = jnp.where(own_i == 0, rows[:tok], rows[tok:])
    send = jnp.where(own_i == 0, rows[tok:], rows[:tok])
    got = pair_swap(send)
    return jnp.where(
        own_i == 0,
        jnp.concatenate([keep, got], axis=1),
        jnp.concatenate([got, keep], axis=1),
    )


def contract_cols(left, right):
    return lax.dot_general(
        left, right, (((1,), (1,)), ((), ())), preferred_element_type=jnp.float32
    )


def contract_rows(left, right):
    return lax.dot_general(
        left, right, (((0,), (0,)), ((), ())), preferred_element_type=jnp.float32
    )


def place_of(routes, own_g, tok, cap):
    mine = (routes.reshape(-1, tok) == own_g).astype(jnp.int32)
    before = jnp.cumsum(mine, axis=1) - mine
    slot = jnp.arange(mine.shape[0], dtype=jnp.int32)[:, None] * cap + before
    return jnp.where(mine == 1, slot, -1).reshape(-1)


def per_device(tokens, routes_f, weight_f, grads, routes_b, weight_b, gate_saved, up_saved,
               gate_proj, up_proj, down_proj):
    tokens, grads = tokens[0], grads[0]
    w_gate, w_up, w_down = gate_proj[0, 0], up_proj[0, 0], down_proj[0, 0]
    devices = lax.axis_size("expert")
    tok = tokens.shape[0]
    slots = gate_saved.shape[1]
    cap = slots // devices
    own = lax.axis_index("expert")
    own_i = own % 2
    own_g = own // 16
    scaled = (weight_b[0] * grads.astype(jnp.float32)).astype(jnp.bfloat16)
    routes = jnp.concatenate([routes_f[0], routes_b[0]], axis=1)
    routes = lax.all_gather(routes, "expert", axis=0, tiled=True)
    place_f = place_of(routes[:, 0], own_g, tok, cap)
    place_b = place_of(routes[:, 1], own_g, tok, cap)
    sel = lambda place: (jnp.arange(slots, dtype=jnp.int32)[:, None] == place[None, :]).astype(jnp.bfloat16)
    sel_f, sel_b = sel(place_f), sel(place_b)

    def gather(rows):
        return lax.all_gather(rows, "expert", axis=0, tiled=True, axis_index_groups=columns())

    def scatter(rows):
        return lax.psum_scatter(rows, "expert", scatter_dimension=0, tiled=True, axis_index_groups=columns())

    all_f = gather(halves(tokens, own_i))
    all_b = gather(halves(scaled, own_i))
    width = w_gate.shape[1]
    pre = jnp.dot(all_f, jnp.concatenate([w_gate, w_up], axis=1), preferred_element_type=jnp.float32)
    pre = jnp.dot(sel_f, pre.astype(jnp.bfloat16), preferred_element_type=jnp.float32)
    pre = pre + pair_swap(pre.astype(jnp.bfloat16)).astype(jnp.float32)
    hidden = (jax.nn.silu(pre[:, :width]) * pre[:, width:]).astype(jnp.bfloat16)
    hidden = contract_rows(sel_f, hidden).astype(jnp.bfloat16)
    out_f = jnp.dot(hidden, w_down, preferred_element_type=jnp.float32).astype(jnp.bfloat16)
    back_f = scatter(out_f)

    down = contract_cols(all_b, w_down)
    down = jnp.dot(sel_b, down.astype(jnp.bfloat16), preferred_element_type=jnp.float32)
    own_kept = jnp.concatenate([gate_saved[0], up_saved[0]], axis=1).astype(jnp.bfloat16)
    other = pair_swap(jnp.concatenate([down.astype(jnp.bfloat16), own_kept], axis=1)).astype(jnp.float32)
    down = down + other[:, :width]
    half = gate_saved.shape[2]

    def joined(mine, theirs):
        return jnp.where(own_i == 0, jnp.concatenate([mine, theirs], 1), jnp.concatenate([theirs, mine], 1))

    a = joined(gate_saved[0], other[:, width:width + half])
    b = joined(up_saved[0], other[:, width + half:])
    p = jax.nn.sigmoid(a)
    d_gate = (down * b * p * (1.0 + a * (1.0 - p))).astype(jnp.bfloat16)
    d_up = (down * a * p).astype(jnp.bfloat16)
    d_both = contract_rows(sel_b, jnp.concatenate([d_gate, d_up], axis=1)).astype(jnp.bfloat16)
    out_b = contract_cols(d_both, jnp.concatenate([w_gate, w_up], axis=1)).astype(jnp.bfloat16)
    back_b = scatter(out_b)

    mixed = (tokens.astype(jnp.float32) + weight_f[0] * rejoin(back_f, own_i).astype(jnp.float32)).astype(jnp.bfloat16)
    grad_in = (grads.astype(jnp.float32) + rejoin(back_b, own_i).astype(jnp.float32)).astype(jnp.bfloat16)
    return from_behind(mixed, "pipe", 1)[None], from_behind(grad_in, "pipe", 1)[None]


def solution(mesh):
    row = P("pipe", "expert", None)
    kept = P("pipe", None, "expert")
    weights = P("pipe", "expert", None, None)
    return jax.shard_map(
        per_device, mesh=mesh,
        in_specs=(row, row, row, row, row, row, kept, kept, weights, weights, weights),
        out_specs=(row, row), check_vma=False)
```

```python
import functools

import jax
import jax.numpy as jnp
from jax import lax
from jax.experimental import pallas as pl
from jax.experimental.pallas import tpu as pltpu
from jax.sharding import PartitionSpec as P

MESH = pl.DeviceIdType.MESH
F32 = jnp.float32
BF16 = jnp.bfloat16
EXT = 128
TOK = 8
CAP = 4
WORK = 15


def nt(left, right):
    return lax.dot_general(left, right, (((1,), (1,)), ((), ())), preferred_element_type=F32)


def nn(left, right):
    return lax.dot_general(left, right, (((1,), (0,)), ((), ())), preferred_element_type=F32)


def kernel(
    ndev, npipe, seg, half, piece,
    full_ref, ext_ref, kept_ref, wg_ref, wu_ref, wd_ref, out_ref,
    agf, agb, rsf, rsb, arrf, arrb, ybuf, graw, xf_send, xf_recv, xb_send, xb_recv,
    kbuf, wcat, wdv, acc, hid, dboth, atok, btok, fin, land,
    ag_send, ag_recv, rs_send, rs_recv, y_send, y_recv, p_send, p_recv, w_sem,
):
    nz = ndev // 2
    far = nz // 2
    rows = ndev * TOK
    slots = ndev * CAP
    pieces = half // piece
    sub_w = half // 2
    pipe = lax.axis_index("pipe")
    me = lax.axis_index("expert")
    own_i = lax.rem(me, 2)
    z = me // 2
    group = z // seg
    partner = me + 1 - 2 * own_i
    right = lax.rem(me + 2, ndev)
    left = lax.rem(me + ndev - 2, ndev)
    ahead = lax.rem(pipe + 1, npipe)
    behind = lax.rem(pipe + npipe - 1, npipe)
    neighbours = ((pipe, left), (pipe, right))

    def chunk_of(index):
        return lax.rem(index + 2 * nz, nz)

    copies = [
        pltpu.make_async_copy(wg_ref, wcat.at[:, pl.ds(0, 128)], w_sem.at[0]),
        pltpu.make_async_copy(wu_ref, wcat.at[:, pl.ds(128, 128)], w_sem.at[1]),
        pltpu.make_async_copy(wd_ref, wdv, w_sem.at[2]),
    ]
    for copy in copies:
        copy.start()

    barrier = pltpu.get_barrier_semaphore()
    for device in (
        (pipe, left), (pipe, right), (pipe, partner), (behind, me), (behind, partner),
    ):
        pl.semaphore_signal(barrier, inc=1, device_id=device, device_id_type=MESH)
    pl.semaphore_wait(barrier, 5)

    def to_partner(src, dst, which):
        return pltpu.make_async_remote_copy(
            src_ref=src, dst_ref=dst, send_sem=y_send.at[which], recv_sem=y_recv.at[which],
            device_id=(pipe, partner), device_id_type=MESH,
        )

    other_cols = pl.ds(pl.multiple_of((1 - own_i) * half, 128), half)
    own_cols = pl.ds(pl.multiple_of(own_i * half, 128), half)
    y_rows = to_partner(full_ref.at[:, other_cols], ybuf.at[:, pl.ds(0, half)], 0)
    y_ext = to_partner(ext_ref, ybuf.at[:, pl.ds(half, EXT)], 1)
    y_kept = to_partner(kept_ref, kbuf, 2)
    y_rows.start()
    y_ext.start()
    y_kept.start()
    y_rows.wait()
    y_ext.wait()

    def in_order(mine, theirs):
        return jnp.where(
            own_i == 0,
            jnp.concatenate([mine, theirs], axis=0),
            jnp.concatenate([theirs, mine], axis=0),
        )

    mine = full_ref[:, own_cols].astype(F32)
    theirs = ybuf[:, 0:half].astype(F32)
    my_ext = ext_ref[...].astype(F32)
    their_ext = ybuf[:, half:half + EXT].astype(F32)
    ext = in_order(my_ext[0:TOK], their_ext[0:TOK])
    w_fwd = ext[:, 32:33] + ext[:, 33:34] + ext[:, 34:35]
    w_bwd = ext[:, 35:36] + ext[:, 36:37] + ext[:, 37:38]
    agf[z, :, 0:half] = in_order(mine[0:TOK], theirs[0:TOK]).astype(BF16)
    agf[z, :, half:half + EXT] = ext.astype(BF16)
    raw = in_order(mine[TOK:], theirs[TOK:])
    graw[...] = raw.astype(BF16)
    agb[z] = (w_bwd * raw).astype(BF16)

    def ag_copy(buf, phase, chunk, way, step, sub):
        start, wide = sub * sub_w, sub_w
        if phase == 0 and sub == 1:
            wide += EXT
        ref = buf.at[chunk, :, pl.ds(start, wide)]
        return pltpu.make_async_remote_copy(
            src_ref=ref, dst_ref=ref,
            send_sem=ag_send.at[phase, way, step, sub], recv_sem=ag_recv.at[phase, chunk, sub],
            device_id=neighbours[way], device_id_type=MESH,
        )

    def ag_begin(buf, phase):
        for sub in (0, 1):
            for way in (1, 0):
                ag_copy(buf, phase, z, way, 0, sub).start()

    def ag_source(way, step):
        return chunk_of(z - step) if way == 1 else chunk_of(z + step)

    def ag_ring(buf, phase, work):
        def body(step, carry):
            for sub in (0, 1):
                for way in (1, 0):
                    copy = ag_copy(buf, phase, ag_source(way, step), way, step, sub)
                    copy.wait_recv()
                    copy.start()
            if work is not None:
                work(step)
            return carry

        lax.fori_loop(1, far - 1, body, 0)
        for sub in (0, 1):
            for way in (1, 0):
                copy = ag_copy(buf, phase, ag_source(way, far - 1), way, far - 1, sub)
                copy.wait_recv()
                if way == 1 - sub:
                    copy.start()

    def ag_end(buf, phase):
        for sub in (0, 1):
            ag_copy(buf, phase, chunk_of(z + far), 0, 0, sub).wait_recv()

    def ag_drain(buf, phase):
        def body(step, carry):
            for sub in (0, 1):
                for way in (1, 0):
                    ag_copy(buf, phase, ag_source(way, step), way, step, sub).wait_send()
            return carry

        lax.fori_loop(0, far - 1, body, 0)
        for sub in (0, 1):
            way = 1 - sub
            ag_copy(buf, phase, ag_source(way, far - 1), way, far - 1, sub).wait_send()

    def cols(index):
        return pl.ds(pl.multiple_of(index * piece, 128), piece)

    def some_pieces(first, act):
        for k in (0, 1):
            index = first + k

            @pl.when(jnp.logical_and(index >= 0, index < pieces))
            def _():
                act(index)

    f_swap = to_partner(xf_send, xf_recv, 3)
    b_swap = to_partner(xb_send, xb_recv, 4)

    def pre_piece(index):
        x = agf[:, :, cols(index)].reshape(rows, piece)
        part = nn(x, wcat[cols(index), :])

        @pl.when(index == 0)
        def _():
            acc[...] = part

        @pl.when(index > 0)
        def _():
            acc[...] += part

    def ext_all():
        return agf[:, :, half:half + EXT].reshape(rows, EXT).astype(F32)

    def place_kept():
        y_kept.wait()
        spot = ext_all()[:, 16:17] - (group * CAP).astype(F32)
        base = ((lax.broadcasted_iota(jnp.int32, (rows, slots), 0) >> 3) * CAP).astype(F32)
        lane = lax.broadcasted_iota(jnp.int32, (rows, slots), 1).astype(F32)
        within = jnp.logical_and(spot >= 0.0, spot < float(CAP))
        target = base + jnp.where(within, spot, -65536.0)
        pick = jnp.where(lane == target, 1.0, 0.0).astype(BF16)
        own = nn(pick, kept_ref[...])
        oth = nn(pick, kbuf[...])
        first = jnp.where(own_i == 0, own, oth)
        second = jnp.where(own_i == 0, oth, own)
        low = lax.broadcasted_iota(jnp.int32, (rows, 128), 1) < 64
        atok[...] = jnp.where(low, first, pltpu.roll(second, 64, 1))
        btok[...] = jnp.where(low, pltpu.roll(first, 64, 1), second)

    def activate():
        f_swap.wait()
        gate = acc[:, 0:128] + xf_recv[:, 0:128].astype(F32)
        upper = acc[:, 128:256] + xf_recv[:, 128:256].astype(F32)
        value = gate * jax.nn.sigmoid(gate) * upper
        mask = ext_all()[:, 0:1] == group.astype(F32)
        hid[...] = jnp.where(mask, value, 0.0).astype(BF16)

    def out_f_piece(index):
        part = nn(hid[...], wdv[:, cols(index)])
        rsf[:, :, cols(index)] = part.astype(BF16).reshape(nz, 16, piece)

    def f_work(step):
        some_pieces(jnp.where(step < 5, (step - 1) * 2, -2), pre_piece)

        @pl.when(step == 4)
        def _():
            xf_send[...] = acc[...].astype(BF16)
            f_swap.start()

        @pl.when(step == 5)
        def _():
            place_kept()

        @pl.when(step == 9)
        def _():
            activate()

        some_pieces(jnp.where(step >= 10, (step - 10) * 2, -2), out_f_piece)

    def down_piece(index):
        x = agb[:, :, cols(index)].reshape(rows, piece)
        part = nt(x, wdv[:, cols(index)])

        @pl.when(index == 0)
        def _():
            acc[:, 0:128] = part

        @pl.when(index > 0)
        def _():
            acc[:, 0:128] += part

    def differentiate():
        b_swap.wait()
        down = acc[:, 0:128] + xb_recv[...].astype(F32)
        a = atok[...]
        p = jax.nn.sigmoid(a)
        dboth[:, 0:128] = (down * btok[...] * p * (1.0 + a * (1.0 - p))).astype(BF16)
        dboth[:, 128:256] = (down * a * p).astype(BF16)

    def out_b_piece(index):
        part = nt(dboth[...], wcat[cols(index), :])
        rsb[:, :, cols(index)] = part.astype(BF16).reshape(nz, 16, piece)

    def b_work(step):
        some_pieces(jnp.where(step < 5, (step - 1) * 2, -2), down_piece)

        @pl.when(step == 4)
        def _():
            xb_send[...] = acc[:, 0:128].astype(BF16)
            b_swap.start()

        @pl.when(step == 8)
        def _():
            differentiate()

        some_pieces(jnp.where(step >= 9, (step - 9) * 2, -2), out_b_piece)

    def leftover(first, work):
        def body(step, carry):
            work(step)
            return carry

        lax.fori_loop(first, WORK, body, 0)

    def rs_dest(way, step):
        return chunk_of(z + far - step) if way == 1 else chunk_of(z - far + step)

    def rs_copy(buf, arr, phase, way, step, sub):
        span = pl.ds(sub * sub_w, sub_w)
        return pltpu.make_async_remote_copy(
            src_ref=buf.at[rs_dest(way, step), :, span], dst_ref=arr.at[way, step, :, span],
            send_sem=rs_send.at[phase, way, step, sub], recv_sem=rs_recv.at[phase, way, step, sub],
            device_id=neighbours[way], device_id_type=MESH,
        )

    def rs_hop(buf, arr, phase, way, step, sub, add):
        if add:
            rs_copy(buf, arr, phase, way, step - 1, sub).wait_recv()
            span = pl.ds(sub * sub_w, sub_w)
            dest = rs_dest(way, step)
            total = buf[dest, :, span].astype(F32) + arr[way, step - 1, :, span].astype(F32)
            buf[dest, :, span] = total.astype(BF16)
        rs_copy(buf, arr, phase, way, step, sub).start()

    def rs_ring(buf, arr, phase, work):
        for sub in (0, 1):
            rs_hop(buf, arr, phase, 1 - sub, 0, sub, False)
        for sub in (0, 1):
            rs_hop(buf, arr, phase, sub, 1, sub, False)
        for sub in (0, 1):
            rs_hop(buf, arr, phase, 1 - sub, 1, sub, True)
        if work is not None:
            work(1)

        def body(step, carry):
            for sub in (0, 1):
                for way in (1, 0):
                    rs_hop(buf, arr, phase, way, step, sub, True)
            if work is not None:
                work(step)
            return carry

        lax.fori_loop(2, far, body, 0)

    def rs_total(buf, arr, phase):
        for way in (1, 0):
            for sub in (0, 1):
                rs_copy(buf, arr, phase, way, far - 1, sub).wait_recv()
        return (
            buf[z].astype(F32) + arr[1, far - 1].astype(F32) + arr[0, far - 1].astype(F32)
        )

    def rs_drain(buf, arr, phase):
        for sub in (0, 1):
            rs_copy(buf, arr, phase, 1 - sub, 0, sub).wait_send()

        def body(step, carry):
            for sub in (0, 1):
                for way in (1, 0):
                    rs_copy(buf, arr, phase, way, step, sub).wait_send()
            return carry

        lax.fori_loop(1, far, body, 0)

    ag_begin(agf, 0)
    for copy in copies:
        copy.wait()
    ag_ring(agf, 0, None)
    ag_begin(agb, 1)
    ag_end(agf, 0)
    ag_ring(agb, 1, f_work)
    leftover(far - 1, f_work)
    ag_end(agb, 1)
    rs_ring(rsf, arrf, 0, b_work)
    leftover(far, b_work)
    ag_drain(agf, 0)
    ag_drain(agb, 1)
    rs_ring(rsb, arrb, 1, None)
    mixed = agf[z, :, 0:half].astype(F32) + w_fwd * rs_total(rsf, arrf, 0)
    grad = graw[...].astype(F32) + rs_total(rsb, arrb, 1)
    for y in (0, 1):
        fin[y] = jnp.concatenate(
            [mixed[y * TOK:(y + 1) * TOK], grad[y * TOK:(y + 1) * TOK]], axis=0
        ).astype(BF16)
    hand = [
        pltpu.make_async_remote_copy(
            src_ref=fin.at[y], dst_ref=land.at[own_i],
            send_sem=p_send.at[y], recv_sem=p_recv.at[own_i],
            device_id=(ahead, z * 2 + y), device_id_type=MESH,
        )
        for y in (0, 1)
    ]
    for copy in hand:
        copy.start()
    rs_drain(rsf, arrf, 0)
    rs_drain(rsb, arrb, 1)
    for copy in hand:
        copy.wait_send()
    for y in (0, 1):
        pltpu.make_async_remote_copy(
            src_ref=fin.at[y], dst_ref=land.at[y],
            send_sem=p_send.at[y], recv_sem=p_recv.at[y],
            device_id=(ahead, me), device_id_type=MESH,
        ).wait_recv()
    out_ref[...] = land[...]


def per_device(npipe, ndev, tokens, routes_f, weight_f, grads, routes_b, weight_b,
               gate_saved, up_saved, gate_proj, up_proj, down_proj):
    half = down_proj.shape[3]
    slots = gate_saved.shape[1]
    rows = ndev * TOK
    nz = ndev // 2
    experts = ndev // min(16, ndev // 2)
    seg = nz // experts
    far = nz // 2
    piece = 512 if half % 512 == 0 else 256

    full = jnp.concatenate([tokens[0], grads[0]], axis=0)
    named = routes_b[0, :, 0]
    order = jnp.arange(TOK, dtype=jnp.int32)
    earlier = jnp.logical_and(named[:, None] == named[None, :], order[None, :] < order[:, None])
    place = named * CAP + jnp.sum(earlier.astype(jnp.int32), axis=1)

    def parts(weight):
        high = lax.reduce_precision(weight, 8, 7)
        middle = lax.reduce_precision(weight - high, 8, 7)
        return [high, middle, weight - high - middle]

    ext = jnp.concatenate(
        [jnp.broadcast_to(routes_f[0].astype(F32), (TOK, 16)),
         jnp.broadcast_to(place[:, None].astype(F32), (TOK, 16))]
        + parts(weight_f[0]) + parts(weight_b[0])
        + [jnp.zeros((TOK, EXT - 38), F32)], axis=1,
    ).astype(BF16)
    ext = jnp.concatenate([ext, ext], axis=0)
    kept = jnp.concatenate([gate_saved[0], up_saved[0]], axis=1).astype(BF16)

    vmem = pl.BlockSpec(memory_space=pltpu.VMEM)
    hbm = pl.BlockSpec(memory_space=pl.ANY)
    V = pltpu.VMEM
    dma = pltpu.SemaphoreType.DMA
    landed = pl.pallas_call(
        functools.partial(kernel, ndev, npipe, seg, half, piece),
        out_shape=jax.ShapeDtypeStruct((2, 16, half), BF16),
        in_specs=[vmem, vmem, vmem, hbm, hbm, hbm],
        out_specs=vmem,
        scratch_shapes=[
            V((nz, 16, half + EXT), BF16),
            V((nz, 16, half), BF16),
            V((nz, 16, half), BF16),
            V((nz, 16, half), BF16),
            V((2, far, 16, half), BF16),
            V((2, far, 16, half), BF16),
            V((16, half + EXT), BF16),
            V((16, half), BF16),
            V((rows, 256), BF16),
            V((rows, 256), BF16),
            V((rows, 128), BF16),
            V((rows, 128), BF16),
            V((slots, 128), BF16),
            V((half, 256), BF16),
            V((128, half), BF16),
            V((rows, 256), F32),
            V((rows, 128), BF16),
            V((rows, 256), BF16),
            V((rows, 128), F32),
            V((rows, 128), F32),
            V((2, 16, half), BF16),
            V((2, 16, half), BF16),
            dma((2, 2, far, 2)),
            dma((2, nz, 2)),
            dma((2, 2, far, 2)),
            dma((2, 2, far, 2)),
            dma((5,)),
            dma((5,)),
            dma((2,)),
            dma((2,)),
            dma((3,)),
        ],
        compiler_params=pltpu.CompilerParams(
            collective_id=0, has_side_effects=True, vmem_limit_bytes=52 * 1024 * 1024
        ),
    )(full, ext, kept, gate_proj[0, 0], up_proj[0, 0], down_proj[0, 0])
    mixed = jnp.concatenate([landed[0, :TOK], landed[1, :TOK]], axis=1)
    grad_in = jnp.concatenate([landed[0, TOK:], landed[1, TOK:]], axis=1)
    return mixed[None], grad_in[None]


def solution(mesh):
    row = P("pipe", "expert", None)
    kept = P("pipe", None, "expert")
    weights = P("pipe", "expert", None, None)
    return jax.shard_map(
        functools.partial(per_device, mesh.shape["pipe"], mesh.shape["expert"]), mesh=mesh,
        in_specs=(row, row, row, row, row, row, kept, kept, weights, weights, weights),
        out_specs=(row, row), check_vma=False,
    )
```

```python
import functools

import jax
import jax.numpy as jnp
from jax import lax
from jax.experimental import pallas as pl
from jax.experimental.pallas import tpu as pltpu
from jax.sharding import PartitionSpec as P

MESH = pl.DeviceIdType.MESH
F32 = jnp.float32
BF16 = jnp.bfloat16
EXT = 128
TOK = 8
CAP = 4
SUBS = 4
LAG = 2


def nt(left, right):
    return lax.dot_general(left, right, (((1,), (1,)), ((), ())), preferred_element_type=F32)


def nn(left, right):
    return lax.dot_general(left, right, (((1,), (0,)), ((), ())), preferred_element_type=F32)


def kernel(
    ndev, npipe, seg, half, piece,
    tok_ref, grd_ref, rf_ref, wf_ref, rb_ref, wb_ref, gk_ref, uk_ref, wg_ref, wu_ref, wd_ref,
    outf_ref, outb_ref,
    agf, agb, rsf, rsb, arrf, arrb, ysf, yrf, ysb, yrb, graw, xf_send, xf_recv, xb_send, xb_recv,
    ksend, kbuf, wcat, wdv, acc, acc_b, hid, dboth, atok, btok, finf, finb, landf, landb,
    ag_send, ag_recv, rs_send, rs_recv, y_send, y_recv, x_send, x_recv, p_send, p_recv, w_sem,
):
    nz = ndev // 2
    far = nz // 2
    lag = min(LAG, far // 4)
    rows = ndev * TOK
    slots = ndev * CAP
    pieces = half // piece
    sub_w = half // SUBS
    quarter = half // 2
    pipe = lax.axis_index("pipe")
    me = lax.axis_index("expert")
    own_i = lax.rem(me, 2)
    z = me // 2
    group = z // seg
    partner = me + 1 - 2 * own_i
    right = lax.rem(me + 2, ndev)
    left = lax.rem(me + ndev - 2, ndev)
    ahead = lax.rem(pipe + 1, npipe)
    behind = lax.rem(pipe + npipe - 1, npipe)
    neighbours = ((pipe, left), (pipe, right))

    def chunk_of(index):
        return lax.rem(index + 2 * nz, nz)

    copies = [
        pltpu.make_async_copy(wg_ref, wcat.at[:, pl.ds(0, 128)], w_sem.at[0]),
        pltpu.make_async_copy(wu_ref, wcat.at[:, pl.ds(128, 128)], w_sem.at[1]),
        pltpu.make_async_copy(wd_ref, wdv, w_sem.at[2]),
    ]
    for copy in copies:
        copy.start()

    barrier = pltpu.get_barrier_semaphore()
    for device in (
        (pipe, left), (pipe, right), (pipe, partner), (behind, me), (behind, partner),
    ):
        pl.semaphore_signal(barrier, inc=1, device_id=device, device_id_type=MESH)

    other_cols = pl.ds(pl.multiple_of((1 - own_i) * half, 128), half)
    own_cols = pl.ds(pl.multiple_of(own_i * half, 128), half)

    def fold(value):
        return jnp.concatenate([value[:, 0:quarter], value[:, quarter:half]], axis=0)

    def unfold(value):
        return jnp.concatenate([value[0:TOK, 0:quarter], value[TOK:16, 0:quarter]], axis=1)

    row8 = lax.broadcasted_iota(jnp.int32, (TOK, TOK), 0)
    col8 = lax.broadcasted_iota(jnp.int32, (TOK, TOK), 1)

    def as_column(row):
        spread = jnp.broadcast_to(row, (TOK, TOK))
        return jnp.sum(jnp.where(row8 == col8, spread, 0.0), axis=1, keepdims=True)

    named_row = rb_ref[...].astype(F32)
    named = as_column(named_row)
    same = jnp.logical_and(named == jnp.broadcast_to(named_row, (TOK, TOK)), col8 < row8)
    place = named * CAP + jnp.sum(jnp.where(same, 1.0, 0.0), axis=1, keepdims=True)
    lanes = lax.broadcasted_iota(jnp.int32, (TOK, EXT), 1)
    own_ext = jnp.where(
        lanes < 16, as_column(rf_ref[...].astype(F32)), jnp.where(lanes < 32, place, 0.0)
    )
    for first, ref in ((32, wf_ref), (35, wb_ref)):
        rest = as_column(ref[...])
        for k in range(3):
            part = rest.astype(BF16).astype(F32)
            own_ext = jnp.where(lanes == first + k, part, own_ext)
            rest = rest - part
    ysf[:, 0:quarter] = fold(tok_ref[:, other_cols].astype(F32)).astype(BF16)
    ysf[:, quarter:quarter + EXT] = jnp.concatenate([own_ext, own_ext], axis=0).astype(BF16)
    ysb[...] = fold(grd_ref[:, other_cols].astype(F32)).astype(BF16)
    ksend[0:64, :] = gk_ref[...].astype(BF16)
    ksend[64:128, :] = uk_ref[...].astype(BF16)
    pl.semaphore_wait(barrier, 5)

    def to_partner(src, dst, which):
        return pltpu.make_async_remote_copy(
            src_ref=src, dst_ref=dst, send_sem=y_send.at[which], recv_sem=y_recv.at[which],
            device_id=(pipe, partner), device_id_type=MESH,
        )

    y_fwd = to_partner(ysf, yrf, 0)
    y_bwd = to_partner(ysb, yrb, 1)
    y_kept = to_partner(ksend, kbuf, 2)
    y_fwd.start()
    y_bwd.start()

    def in_order(mine, theirs):
        return jnp.where(
            own_i == 0,
            jnp.concatenate([mine, theirs], axis=0),
            jnp.concatenate([theirs, mine], axis=0),
        )

    def ag_copy(buf, phase, chunk, way, step, sub):
        start, wide = sub * sub_w, sub_w
        if phase == 0 and sub == SUBS - 1:
            wide += EXT
        ref = buf.at[chunk, :, pl.ds(start, wide)]
        return pltpu.make_async_remote_copy(
            src_ref=ref, dst_ref=ref,
            send_sem=ag_send.at[phase, way, step, sub], recv_sem=ag_recv.at[phase, chunk, sub],
            device_id=neighbours[way], device_id_type=MESH,
        )

    def last_way(sub):
        return 1 if sub < SUBS // 2 else 0

    def ag_begin(buf, phase):
        for sub in range(SUBS):
            for way in (1, 0):
                ag_copy(buf, phase, z, way, 0, sub).start()

    def ag_source(way, step):
        return chunk_of(z - step) if way == 1 else chunk_of(z + step)

    def ag_hop(buf, phase, step, act):
        for sub in range(SUBS):
            for way in (1, 0):
                copy = ag_copy(buf, phase, ag_source(way, step), way, step, sub)
                copy.wait_recv()
                copy.start()
            act(step, sub)

    def ag_any(buf, phase, step, act):
        if step < far - 1:
            ag_hop(buf, phase, step, act)
        elif step == far - 1:
            for sub in range(SUBS):
                for way in (1, 0):
                    copy = ag_copy(buf, phase, ag_source(way, step), way, step, sub)
                    copy.wait_recv()
                    if way == last_way(sub):
                        copy.start()
                act(step, sub)
        elif step == far:
            for sub in range(SUBS):
                ag_copy(buf, phase, chunk_of(z + far), 0, 0, sub).wait_recv()
                act(step, sub)

    def ag_drain(buf, phase):
        def body(step, carry):
            for sub in range(SUBS):
                for way in (1, 0):
                    ag_copy(buf, phase, ag_source(way, step), way, step, sub).wait_send()
            return carry

        lax.fori_loop(0, far - 1, body, 0)
        for sub in range(SUBS):
            way = last_way(sub)
            ag_copy(buf, phase, ag_source(way, far - 1), way, far - 1, sub).wait_send()

    def cols(index):
        return pl.ds(pl.multiple_of(index * piece, 128), piece)

    def all_pieces(act):
        def body(index, carry):
            act(index)
            return carry

        lax.fori_loop(0, pieces, body, 0)

    def rows_of(buf, step, sub):
        first = chunk_of(z - step)
        second = chunk_of(z + step)
        if isinstance(step, int) and step == far:
            second = z
        span = pl.ds(sub * sub_w, sub_w)
        return first, second, jnp.concatenate([buf[first, :, span], buf[second, :, span]], axis=0)

    def gather_into(total, first, second, part, sub):
        if sub == 0:
            total[first] = part[0:16]
            total[second] = part[16:32]
        else:
            total[first] += part[0:16]
            total[second] += part[16:32]

    def swap(phase, chunk):
        src, dst = (xf_send, xf_recv) if phase == 0 else (xb_send, xb_recv)
        return pltpu.make_async_remote_copy(
            src_ref=src.at[chunk], dst_ref=dst.at[chunk],
            send_sem=x_send.at[phase, chunk], recv_sem=x_recv.at[phase, chunk],
            device_id=(pipe, partner), device_id_type=MESH,
        )

    def swap_rows(phase, chunks):
        src, dst = (acc, xf_send) if phase == 0 else (acc_b, xb_send)
        for chunk in chunks:
            dst[chunk] = src[chunk].astype(BF16)
            swap(phase, chunk).start()

    def swap_wait(phase):
        def body(chunk, carry):
            swap(phase, chunk).wait()
            return carry

        lax.fori_loop(0, nz, body, 0)

    def pre_rows(step, sub):
        first, second, x = rows_of(agf, step, sub)
        part = nn(x, wcat[sub * sub_w:(sub + 1) * sub_w, :])
        gather_into(acc, first, second, part, sub)
        if sub == SUBS - 1:
            swap_rows(0, (first, second))

    def down_rows(step, sub):
        first, second, x = rows_of(agb, step, sub)
        part = nt(x, wdv[:, sub * sub_w:(sub + 1) * sub_w])
        gather_into(acc_b, first, second, part, sub)
        if sub == SUBS - 1:
            swap_rows(1, (first, second))

    def ext_all():
        return agf[:, :, half:half + EXT].reshape(rows, EXT).astype(F32)

    def place_kept():
        y_kept.wait()
        spot = ext_all()[:, 16:17] - (group * CAP).astype(F32)
        base = ((lax.broadcasted_iota(jnp.int32, (rows, slots), 0) >> 3) * CAP).astype(F32)
        lane = lax.broadcasted_iota(jnp.int32, (rows, slots), 1).astype(F32)
        within = jnp.logical_and(spot >= 0.0, spot < float(CAP))
        target = base + jnp.where(within, spot, -65536.0)
        pick = jnp.where(lane == target, 1.0, 0.0).astype(BF16)
        own = nt(pick, ksend[...])
        oth = nt(pick, kbuf[...])
        first = jnp.where(own_i == 0, own, oth)
        second = jnp.where(own_i == 0, oth, own)
        low = lax.broadcasted_iota(jnp.int32, (rows, 128), 1) < 64
        atok[...] = jnp.where(low, first, pltpu.roll(second, 64, 1))
        btok[...] = jnp.where(low, pltpu.roll(first, 64, 1), second)

    def activate():
        swap_wait(0)
        both = (acc[...] + xf_recv[...].astype(F32)).reshape(rows, 256)
        gate = both[:, 0:128]
        upper = both[:, 128:256]
        value = gate * jax.nn.sigmoid(gate) * upper
        mask = ext_all()[:, 0:1] == group.astype(F32)
        hid[...] = jnp.where(mask, value, 0.0).astype(BF16)

    def out_f_piece(index):
        part = nn(hid[...], wdv[:, cols(index)])
        rsf[:, :, cols(index)] = part.astype(BF16).reshape(nz, 16, piece)

    def differentiate():
        swap_wait(1)
        down = (acc_b[...] + xb_recv[...].astype(F32)).reshape(rows, 128)
        a = atok[...]
        p = jax.nn.sigmoid(a)
        dboth[:, 0:128] = (down * btok[...] * p * (1.0 + a * (1.0 - p))).astype(BF16)
        dboth[:, 128:256] = (down * a * p).astype(BF16)

    def out_b_piece(index):
        part = nt(dboth[...], wcat[cols(index), :])
        rsb[:, :, cols(index)] = part.astype(BF16).reshape(nz, 16, piece)

    def rs_dest(way, step):
        return chunk_of(z + far - step) if way == 1 else chunk_of(z - far + step)

    def rs_copy(buf, arr, phase, way, step, sub):
        span = pl.ds(sub * sub_w, sub_w)
        return pltpu.make_async_remote_copy(
            src_ref=buf.at[rs_dest(way, step), :, span], dst_ref=arr.at[way, step, :, span],
            send_sem=rs_send.at[phase, way, step, sub], recv_sem=rs_recv.at[phase, way, step, sub],
            device_id=neighbours[way], device_id_type=MESH,
        )

    def rs_hop(buf, arr, phase, way, step, sub, add):
        if add:
            rs_copy(buf, arr, phase, way, step - 1, sub).wait_recv()
            span = pl.ds(sub * sub_w, sub_w)
            dest = rs_dest(way, step)
            total = buf[dest, :, span].astype(F32) + arr[way, step - 1, :, span].astype(F32)
            buf[dest, :, span] = total.astype(BF16)
        rs_copy(buf, arr, phase, way, step, sub).start()

    def rs_step(buf, arr, phase, step):
        order = [(sub, way) for sub in range(SUBS) for way in (1, 0)]
        if isinstance(step, int) and step < 2:
            late = [(sub, way) for sub, way in order if way != last_way(sub)]
            early = [(sub, way) for sub, way in order if way == last_way(sub)]
            if step == 1:
                for sub, way in late:
                    rs_hop(buf, arr, phase, way, step, sub, False)
            for sub, way in early:
                rs_hop(buf, arr, phase, way, step, sub, step == 1)
        else:
            for sub, way in order:
                rs_hop(buf, arr, phase, way, step, sub, True)

    def rs_total(buf, arr, phase):
        for way in (1, 0):
            for sub in range(SUBS):
                rs_copy(buf, arr, phase, way, far - 1, sub).wait_recv()
        return (
            buf[z].astype(F32) + arr[1, far - 1].astype(F32) + arr[0, far - 1].astype(F32)
        )

    def rs_drain(buf, arr, phase):
        for sub in range(SUBS):
            rs_copy(buf, arr, phase, last_way(sub), 0, sub).wait_send()

        def body(step, carry):
            for sub in range(SUBS):
                for way in (1, 0):
                    rs_copy(buf, arr, phase, way, step, sub).wait_send()
            return carry

        lax.fori_loop(1, far, body, 0)

    def loop(first, last, act):
        def body(step, carry):
            act(step)
            return carry

        lax.fori_loop(first, last, body, 0)

    y_fwd.wait()
    theirs = yrf[...].astype(F32)
    ext = in_order(own_ext, theirs[0:TOK, quarter:quarter + EXT])
    agf[z, :, 0:half] = in_order(tok_ref[:, own_cols].astype(F32), unfold(theirs)).astype(BF16)
    agf[z, :, half:half + EXT] = ext.astype(BF16)
    ag_begin(agf, 0)
    w_fwd = ext[:, 32:33] + ext[:, 33:34] + ext[:, 34:35]
    w_bwd = ext[:, 35:36] + ext[:, 36:37] + ext[:, 37:38]
    y_bwd.wait()
    y_kept.start()
    raw = in_order(grd_ref[:, own_cols].astype(F32), unfold(yrb[...].astype(F32)))
    graw[...] = raw.astype(BF16)
    agb[z] = (w_bwd * raw).astype(BF16)
    for copy in copies:
        copy.wait()
    loop(1, lag + 1, lambda step: ag_hop(agf, 0, step, pre_rows))
    ag_begin(agb, 1)

    def both_gather(step):
        ag_hop(agf, 0, step, pre_rows)
        ag_hop(agb, 1, step - lag, down_rows)

    loop(lag + 1, far - 1, both_gather)
    ag_any(agf, 0, far - 1, pre_rows)
    ag_any(agb, 1, far - 1 - lag, down_rows)
    ag_any(agf, 0, far, pre_rows)
    tasks = [place_kept, activate, lambda: all_pieces(out_f_piece)]
    for step in range(far - lag, far):
        ag_any(agb, 1, step, down_rows)
        if tasks:
            tasks.pop(0)()
    while tasks:
        tasks.pop(0)()
    rs_step(rsf, arrf, 0, 0)
    ag_any(agb, 1, far, down_rows)
    tasks = [differentiate, lambda: all_pieces(out_b_piece)]
    for step in range(1, lag):
        rs_step(rsf, arrf, 0, step)
        if tasks:
            tasks.pop(0)()
    while tasks:
        tasks.pop(0)()
    for step in (lag, lag + 1):
        rs_step(rsf, arrf, 0, step)
        rs_step(rsb, arrb, 1, step - lag)

    def both_reduce(step):
        rs_step(rsf, arrf, 0, step)
        rs_step(rsb, arrb, 1, step - lag)

    loop(lag + 2, far, both_reduce)
    def hand(phase, fin, land, y, slot):
        return pltpu.make_async_remote_copy(
            src_ref=fin.at[y], dst_ref=land.at[slot],
            send_sem=p_send.at[phase, y], recv_sem=p_recv.at[phase, slot],
            device_id=(ahead, z * 2 + y), device_id_type=MESH,
        )

    def give(phase, fin, land, value):
        for y in (0, 1):
            fin[y] = fold(value[y * TOK:(y + 1) * TOK]).astype(BF16)
            hand(phase, fin, land, y, own_i).start()

    def take(phase, fin, land, out):
        for y in (0, 1):
            hand(phase, fin, land, y, y).wait_recv()
            hand(phase, fin, land, y, own_i).wait_send()
            out[:, y * half:(y + 1) * half] = unfold(land[y].astype(F32)).astype(BF16)

    rs_step(rsb, arrb, 1, far - lag)
    give(0, finf, landf, agf[z, :, 0:half].astype(F32) + w_fwd * rs_total(rsf, arrf, 0))
    loop(far - lag + 1, far, lambda step: rs_step(rsb, arrb, 1, step))
    ag_drain(agf, 0)
    ag_drain(agb, 1)
    rs_drain(rsf, arrf, 0)
    take(0, finf, landf, outf_ref)
    give(1, finb, landb, graw[...].astype(F32) + rs_total(rsb, arrb, 1))
    rs_drain(rsb, arrb, 1)
    take(1, finb, landb, outb_ref)


def per_device(npipe, ndev, tokens, routes_f, weight_f, grads, routes_b, weight_b,
               gate_saved, up_saved, gate_proj, up_proj, down_proj):
    half = down_proj.shape[3]
    slots = gate_saved.shape[1]
    rows = ndev * TOK
    nz = ndev // 2
    experts = ndev // min(16, ndev // 2)
    seg = nz // experts
    far = nz // 2
    piece = 512 if half % 512 == 0 else 256

    def flat(value):
        return value[0].reshape(1, TOK)

    kept_gate, kept_up = gate_saved[0].T, up_saved[0].T
    vmem = pl.BlockSpec(memory_space=pltpu.VMEM)
    hbm = pl.BlockSpec(memory_space=pl.ANY)
    V = pltpu.VMEM
    dma = pltpu.SemaphoreType.DMA
    outs = pl.pallas_call(
        functools.partial(kernel, ndev, npipe, seg, half, piece),
        out_shape=[jax.ShapeDtypeStruct((TOK, 2 * half), BF16)] * 2,
        in_specs=[vmem] * 8 + [hbm] * 3,
        out_specs=[vmem] * 2,
        scratch_shapes=[
            V((nz, 16, half + EXT), BF16),
            V((nz, 16, half), BF16),
            V((nz, 16, half), BF16),
            V((nz, 16, half), BF16),
            V((2, far, 16, half), BF16),
            V((2, far, 16, half), BF16),
            V((16, half // 2 + EXT), BF16),
            V((16, half // 2 + EXT), BF16),
            V((16, half // 2), BF16),
            V((16, half // 2), BF16),
            V((16, half), BF16),
            V((nz, 16, 256), BF16),
            V((nz, 16, 256), BF16),
            V((nz, 16, 128), BF16),
            V((nz, 16, 128), BF16),
            V((128, slots), BF16),
            V((128, slots), BF16),
            V((half, 256), BF16),
            V((128, half), BF16),
            V((nz, 16, 256), F32),
            V((nz, 16, 128), F32),
            V((rows, 128), BF16),
            V((rows, 256), BF16),
            V((rows, 128), F32),
            V((rows, 128), F32),
            V((2, 16, half // 2), BF16),
            V((2, 16, half // 2), BF16),
            V((2, 16, half // 2), BF16),
            V((2, 16, half // 2), BF16),
            dma((2, 2, far, SUBS)),
            dma((2, nz, SUBS)),
            dma((2, 2, far, SUBS)),
            dma((2, 2, far, SUBS)),
            dma((3,)),
            dma((3,)),
            dma((2, nz)),
            dma((2, nz)),
            dma((2, 2)),
            dma((2, 2)),
            dma((3,)),
        ],
        compiler_params=pltpu.CompilerParams(
            collective_id=0, has_side_effects=True, vmem_limit_bytes=52 * 1024 * 1024
        ),
    )(
        tokens[0], grads[0], flat(routes_f), flat(weight_f), flat(routes_b), flat(weight_b),
        kept_gate, kept_up, gate_proj[0, 0], up_proj[0, 0], down_proj[0, 0],
    )
    return outs[0][None], outs[1][None]


def solution(mesh):
    row = P("pipe", "expert", None)
    kept = P("pipe", None, "expert")
    weights = P("pipe", "expert", None, None)
    return jax.shard_map(
        functools.partial(per_device, mesh.shape["pipe"], mesh.shape["expert"]), mesh=mesh,
        in_specs=(row, row, row, row, row, row, kept, kept, weights, weights, weights),
        out_specs=(row, row), check_vma=False,
    )
```

```python
import functools

import jax
import jax.numpy as jnp
from jax import lax
from jax.experimental import pallas as pl
from jax.experimental.pallas import tpu as pltpu
from jax.sharding import PartitionSpec as P

MESH = pl.DeviceIdType.MESH
F32 = jnp.float32
BF16 = jnp.bfloat16
EXT = 128
TOK = 8
CAP = 4
SUBS = 4
LAG = 2


def nt(left, right):
    return lax.dot_general(left, right, (((1,), (1,)), ((), ())), preferred_element_type=F32)


def nn(left, right):
    return lax.dot_general(left, right, (((1,), (0,)), ((), ())), preferred_element_type=F32)


def kernel(
    ndev, npipe, seg, half, piece,
    tok_hbm, grd_hbm, rf_ref, wf_ref, rb_ref, wb_ref, gk_hbm, uk_hbm, wg_ref, wu_ref, wd_ref,
    outf_ref, outb_ref,
    tok_ref, grd_ref, gk_ref, uk_ref, agf, agb, rsf, rsb, arrf, arrb, ysf, yrf, ysb, yrb, graw, xf_send, xf_recv, xb_send, xb_recv,
    ksend, kbuf, wcat, wdv, acc, acc_b, hid, dboth, atok, btok, finf, finb, landf, landb,
    ag_send, ag_recv, rs_send, rs_recv, y_send, y_recv, x_send, x_recv, p_send, p_recv, w_sem,
):
    nz = ndev // 2
    far = nz // 2
    lag = min(LAG, far // 4)
    rows = ndev * TOK
    slots = ndev * CAP
    pieces = half // piece
    sub_w = half // SUBS
    quarter = half // 2
    pipe = lax.axis_index("pipe")
    me = lax.axis_index("expert")
    own_i = lax.rem(me, 2)
    z = me // 2
    group = z // seg
    partner = me + 1 - 2 * own_i
    right = lax.rem(me + 2, ndev)
    left = lax.rem(me + ndev - 2, ndev)
    ahead = lax.rem(pipe + 1, npipe)
    behind = lax.rem(pipe + npipe - 1, npipe)
    neighbours = ((pipe, left), (pipe, right))

    def chunk_of(index):
        return lax.rem(index + 2 * nz, nz)

    early = [
        pltpu.make_async_copy(src, dst, w_sem.at[3 + k])
        for k, (src, dst) in enumerate(
            ((tok_hbm, tok_ref), (grd_hbm, grd_ref), (gk_hbm, gk_ref), (uk_hbm, uk_ref))
        )
    ]
    for copy in early:
        copy.start()
    copies = [
        pltpu.make_async_copy(wg_ref, wcat.at[:, pl.ds(0, 128)], w_sem.at[0]),
        pltpu.make_async_copy(wu_ref, wcat.at[:, pl.ds(128, 128)], w_sem.at[1]),
        pltpu.make_async_copy(wd_ref, wdv, w_sem.at[2]),
    ]
    barrier = pltpu.get_barrier_semaphore()
    for device in (
        (pipe, left), (pipe, right), (pipe, partner), (behind, me), (behind, partner),
    ):
        pl.semaphore_signal(barrier, inc=1, device_id=device, device_id_type=MESH)

    other_cols = pl.ds(pl.multiple_of((1 - own_i) * half, 128), half)
    own_cols = pl.ds(pl.multiple_of(own_i * half, 128), half)

    def fold(value):
        return jnp.concatenate([value[:, 0:quarter], value[:, quarter:half]], axis=0)

    def unfold(value):
        return jnp.concatenate([value[0:TOK, 0:quarter], value[TOK:16, 0:quarter]], axis=1)

    row8 = lax.broadcasted_iota(jnp.int32, (TOK, TOK), 0)
    col8 = lax.broadcasted_iota(jnp.int32, (TOK, TOK), 1)

    def as_column(row):
        spread = jnp.broadcast_to(row, (TOK, TOK))
        return jnp.sum(jnp.where(row8 == col8, spread, 0.0), axis=1, keepdims=True)

    for copy in copies:
        copy.start()
    named_row = rb_ref[...].astype(F32)
    named = as_column(named_row)
    same = jnp.logical_and(named == jnp.broadcast_to(named_row, (TOK, TOK)), col8 < row8)
    place = named * CAP + jnp.sum(jnp.where(same, 1.0, 0.0), axis=1, keepdims=True)
    lanes = lax.broadcasted_iota(jnp.int32, (TOK, EXT), 1)
    own_ext = jnp.where(
        lanes < 16, as_column(rf_ref[...].astype(F32)), jnp.where(lanes < 32, place, 0.0)
    )
    for first, ref in ((32, wf_ref), (35, wb_ref)):
        rest = as_column(ref[...])
        for k in range(3):
            part = rest.astype(BF16).astype(F32)
            own_ext = jnp.where(lanes == first + k, part, own_ext)
            rest = rest - part
    early[0].wait()
    ysf[:, 0:quarter] = fold(tok_ref[:, other_cols].astype(F32)).astype(BF16)
    ysf[:, quarter:quarter + EXT] = jnp.concatenate([own_ext, own_ext], axis=0).astype(BF16)
    early[1].wait()
    ysb[...] = fold(grd_ref[:, other_cols].astype(F32)).astype(BF16)
    pl.semaphore_wait(barrier, 5)

    def to_partner(src, dst, which):
        return pltpu.make_async_remote_copy(
            src_ref=src, dst_ref=dst, send_sem=y_send.at[which], recv_sem=y_recv.at[which],
            device_id=(pipe, partner), device_id_type=MESH,
        )

    y_fwd = to_partner(ysf, yrf, 0)
    y_bwd = to_partner(ysb, yrb, 1)
    y_kept = to_partner(ksend, kbuf, 2)
    y_fwd.start()
    y_bwd.start()
    early[2].wait()
    early[3].wait()
    ksend[0:64, :] = gk_ref[...].astype(BF16)
    ksend[64:128, :] = uk_ref[...].astype(BF16)

    def in_order(mine, theirs):
        return jnp.where(
            own_i == 0,
            jnp.concatenate([mine, theirs], axis=0),
            jnp.concatenate([theirs, mine], axis=0),
        )

    def ag_copy(buf, phase, chunk, way, step, sub):
        start, wide = sub * sub_w, sub_w
        if phase == 0 and sub == SUBS - 1:
            wide += EXT
        ref = buf.at[chunk, :, pl.ds(start, wide)]
        return pltpu.make_async_remote_copy(
            src_ref=ref, dst_ref=ref,
            send_sem=ag_send.at[phase, way, step, sub], recv_sem=ag_recv.at[phase, chunk, sub],
            device_id=neighbours[way], device_id_type=MESH,
        )

    def last_way(sub):
        return 1 if sub < SUBS // 2 else 0

    def ag_begin(buf, phase):
        for sub in range(SUBS):
            for way in (1, 0):
                ag_copy(buf, phase, z, way, 0, sub).start()

    def ag_source(way, step):
        return chunk_of(z - step) if way == 1 else chunk_of(z + step)

    def ag_hop(buf, phase, step, act):
        for sub in range(SUBS):
            for way in (1, 0):
                copy = ag_copy(buf, phase, ag_source(way, step), way, step, sub)
                copy.wait_recv()
                copy.start()
            act(step, sub)

    def ag_any(buf, phase, step, act):
        if step < far - 1:
            ag_hop(buf, phase, step, act)
        elif step == far - 1:
            for sub in range(SUBS):
                for way in (1, 0):
                    copy = ag_copy(buf, phase, ag_source(way, step), way, step, sub)
                    copy.wait_recv()
                    if way == last_way(sub):
                        copy.start()
                act(step, sub)
        elif step == far:
            for sub in range(SUBS):
                ag_copy(buf, phase, chunk_of(z + far), 0, 0, sub).wait_recv()
                act(step, sub)

    def ag_drain(buf, phase):
        def body(step, carry):
            for sub in range(SUBS):
                for way in (1, 0):
                    ag_copy(buf, phase, ag_source(way, step), way, step, sub).wait_send()
            return carry

        lax.fori_loop(0, far - 1, body, 0)
        for sub in range(SUBS):
            way = last_way(sub)
            ag_copy(buf, phase, ag_source(way, far - 1), way, far - 1, sub).wait_send()

    def cols(index):
        return pl.ds(pl.multiple_of(index * piece, 128), piece)

    def all_pieces(act):
        def body(index, carry):
            act(index)
            return carry

        lax.fori_loop(0, pieces, body, 0)

    def rows_of(buf, step, sub):
        first = chunk_of(z - step)
        second = chunk_of(z + step)
        if isinstance(step, int) and step == far:
            second = z
        span = pl.ds(sub * sub_w, sub_w)
        return first, second, jnp.concatenate([buf[first, :, span], buf[second, :, span]], axis=0)

    def gather_into(total, first, second, part, sub):
        if sub == 0:
            total[first] = part[0:16]
            total[second] = part[16:32]
        else:
            total[first] += part[0:16]
            total[second] += part[16:32]

    def swap(phase, chunk):
        src, dst = (xf_send, xf_recv) if phase == 0 else (xb_send, xb_recv)
        return pltpu.make_async_remote_copy(
            src_ref=src.at[chunk], dst_ref=dst.at[chunk],
            send_sem=x_send.at[phase, chunk], recv_sem=x_recv.at[phase, chunk],
            device_id=(pipe, partner), device_id_type=MESH,
        )

    def swap_rows(phase, chunks):
        src, dst = (acc, xf_send) if phase == 0 else (acc_b, xb_send)
        for chunk in chunks:
            dst[chunk] = src[chunk].astype(BF16)
            swap(phase, chunk).start()

    def swap_wait(phase):
        def body(chunk, carry):
            swap(phase, chunk).wait()
            return carry

        lax.fori_loop(0, nz, body, 0)

    def pre_rows(step, sub):
        first, second, x = rows_of(agf, step, sub)
        part = nn(x, wcat[sub * sub_w:(sub + 1) * sub_w, :])
        gather_into(acc, first, second, part, sub)
        if sub == SUBS - 1:
            swap_rows(0, (first, second))

    def down_rows(step, sub):
        first, second, x = rows_of(agb, step, sub)
        part = nt(x, wdv[:, sub * sub_w:(sub + 1) * sub_w])
        gather_into(acc_b, first, second, part, sub)
        if sub == SUBS - 1:
            swap_rows(1, (first, second))

    def ext_all():
        return agf[:, :, half:half + EXT].reshape(rows, EXT).astype(F32)

    def place_kept():
        y_kept.wait()
        spot = ext_all()[:, 16:17] - (group * CAP).astype(F32)
        base = ((lax.broadcasted_iota(jnp.int32, (rows, slots), 0) >> 3) * CAP).astype(F32)
        lane = lax.broadcasted_iota(jnp.int32, (rows, slots), 1).astype(F32)
        within = jnp.logical_and(spot >= 0.0, spot < float(CAP))
        target = base + jnp.where(within, spot, -65536.0)
        pick = jnp.where(lane == target, 1.0, 0.0).astype(BF16)
        own = nt(pick, ksend[...])
        oth = nt(pick, kbuf[...])
        first = jnp.where(own_i == 0, own, oth)
        second = jnp.where(own_i == 0, oth, own)
        low = lax.broadcasted_iota(jnp.int32, (rows, 128), 1) < 64
        atok[...] = jnp.where(low, first, pltpu.roll(second, 64, 1))
        btok[...] = jnp.where(low, pltpu.roll(first, 64, 1), second)

    def activate():
        swap_wait(0)
        both = (acc[...] + xf_recv[...].astype(F32)).reshape(rows, 256)
        gate = both[:, 0:128]
        upper = both[:, 128:256]
        value = gate * jax.nn.sigmoid(gate) * upper
        mask = ext_all()[:, 0:1] == group.astype(F32)
        hid[...] = jnp.where(mask, value, 0.0).astype(BF16)

    def out_f_piece(index):
        part = nn(hid[...], wdv[:, cols(index)])
        rsf[:, :, cols(index)] = part.astype(BF16).reshape(nz, 16, piece)

    def differentiate():
        swap_wait(1)
        down = (acc_b[...] + xb_recv[...].astype(F32)).reshape(rows, 128)
        a = atok[...]
        p = jax.nn.sigmoid(a)
        dboth[:, 0:128] = (down * btok[...] * p * (1.0 + a * (1.0 - p))).astype(BF16)
        dboth[:, 128:256] = (down * a * p).astype(BF16)

    def out_b_piece(index):
        part = nt(dboth[...], wcat[cols(index), :])
        rsb[:, :, cols(index)] = part.astype(BF16).reshape(nz, 16, piece)

    def rs_dest(way, step):
        return chunk_of(z + far - step) if way == 1 else chunk_of(z - far + step)

    def rs_copy(buf, arr, phase, way, step, sub):
        span = pl.ds(sub * sub_w, sub_w)
        return pltpu.make_async_remote_copy(
            src_ref=buf.at[rs_dest(way, step), :, span], dst_ref=arr.at[way, step, :, span],
            send_sem=rs_send.at[phase, way, step, sub], recv_sem=rs_recv.at[phase, way, step, sub],
            device_id=neighbours[way], device_id_type=MESH,
        )

    def rs_hop(buf, arr, phase, way, step, sub, add):
        if add:
            rs_copy(buf, arr, phase, way, step - 1, sub).wait_recv()
            span = pl.ds(sub * sub_w, sub_w)
            dest = rs_dest(way, step)
            total = buf[dest, :, span].astype(F32) + arr[way, step - 1, :, span].astype(F32)
            buf[dest, :, span] = total.astype(BF16)
        rs_copy(buf, arr, phase, way, step, sub).start()

    def rs_step(buf, arr, phase, step):
        order = [(sub, way) for sub in range(SUBS) for way in (1, 0)]
        if isinstance(step, int) and step < 2:
            late = [(sub, way) for sub, way in order if way != last_way(sub)]
            early = [(sub, way) for sub, way in order if way == last_way(sub)]
            if step == 1:
                for sub, way in late:
                    rs_hop(buf, arr, phase, way, step, sub, False)
            for sub, way in early:
                rs_hop(buf, arr, phase, way, step, sub, step == 1)
        else:
            for sub, way in order:
                rs_hop(buf, arr, phase, way, step, sub, True)

    def rs_total(buf, arr, phase):
        for way in (1, 0):
            for sub in range(SUBS):
                rs_copy(buf, arr, phase, way, far - 1, sub).wait_recv()
        return (
            buf[z].astype(F32) + arr[1, far - 1].astype(F32) + arr[0, far - 1].astype(F32)
        )

    def rs_drain(buf, arr, phase):
        for sub in range(SUBS):
            rs_copy(buf, arr, phase, last_way(sub), 0, sub).wait_send()

        def body(step, carry):
            for sub in range(SUBS):
                for way in (1, 0):
                    rs_copy(buf, arr, phase, way, step, sub).wait_send()
            return carry

        lax.fori_loop(1, far, body, 0)

    def loop(first, last, act):
        def body(step, carry):
            act(step)
            return carry

        lax.fori_loop(first, last, body, 0)

    y_fwd.wait()
    theirs = yrf[...].astype(F32)
    ext = in_order(own_ext, theirs[0:TOK, quarter:quarter + EXT])
    agf[z, :, 0:half] = in_order(tok_ref[:, own_cols].astype(F32), unfold(theirs)).astype(BF16)
    agf[z, :, half:half + EXT] = ext.astype(BF16)
    ag_begin(agf, 0)
    w_fwd = ext[:, 32:33] + ext[:, 33:34] + ext[:, 34:35]
    w_bwd = ext[:, 35:36] + ext[:, 36:37] + ext[:, 37:38]
    y_bwd.wait()
    y_kept.start()
    raw = in_order(grd_ref[:, own_cols].astype(F32), unfold(yrb[...].astype(F32)))
    graw[...] = raw.astype(BF16)
    agb[z] = (w_bwd * raw).astype(BF16)
    for copy in copies:
        copy.wait()
    loop(1, lag + 1, lambda step: ag_hop(agf, 0, step, pre_rows))
    ag_begin(agb, 1)

    def both_gather(step):
        ag_hop(agf, 0, step, pre_rows)
        ag_hop(agb, 1, step - lag, down_rows)

    loop(lag + 1, far - 1, both_gather)
    ag_any(agf, 0, far - 1, pre_rows)
    ag_any(agb, 1, far - 1 - lag, down_rows)
    ag_any(agf, 0, far, pre_rows)
    tasks = [place_kept, activate, lambda: all_pieces(out_f_piece)]
    for step in range(far - lag, far):
        ag_any(agb, 1, step, down_rows)
        if tasks:
            tasks.pop(0)()
    while tasks:
        tasks.pop(0)()
    rs_step(rsf, arrf, 0, 0)
    ag_any(agb, 1, far, down_rows)
    tasks = [differentiate, lambda: all_pieces(out_b_piece)]
    for step in range(1, lag):
        rs_step(rsf, arrf, 0, step)
        if tasks:
            tasks.pop(0)()
    while tasks:
        tasks.pop(0)()
    for step in (lag, lag + 1):
        rs_step(rsf, arrf, 0, step)
        rs_step(rsb, arrb, 1, step - lag)

    def both_reduce(step):
        rs_step(rsf, arrf, 0, step)
        rs_step(rsb, arrb, 1, step - lag)

    loop(lag + 2, far, both_reduce)
    def hand(phase, fin, land, y, slot):
        return pltpu.make_async_remote_copy(
            src_ref=fin.at[y], dst_ref=land.at[slot],
            send_sem=p_send.at[phase, y], recv_sem=p_recv.at[phase, slot],
            device_id=(ahead, z * 2 + y), device_id_type=MESH,
        )

    def give(phase, fin, land, value):
        for y in (0, 1):
            fin[y] = fold(value[y * TOK:(y + 1) * TOK]).astype(BF16)
            hand(phase, fin, land, y, own_i).start()

    def take(phase, fin, land, out):
        for y in (0, 1):
            hand(phase, fin, land, y, y).wait_recv()
            hand(phase, fin, land, y, own_i).wait_send()
            out[:, y * half:(y + 1) * half] = unfold(land[y].astype(F32)).astype(BF16)

    rs_step(rsb, arrb, 1, far - lag)
    give(0, finf, landf, agf[z, :, 0:half].astype(F32) + w_fwd * rs_total(rsf, arrf, 0))
    loop(far - lag + 1, far, lambda step: rs_step(rsb, arrb, 1, step))
    ag_drain(agf, 0)
    ag_drain(agb, 1)
    rs_drain(rsf, arrf, 0)
    take(0, finf, landf, outf_ref)
    give(1, finb, landb, graw[...].astype(F32) + rs_total(rsb, arrb, 1))
    rs_drain(rsb, arrb, 1)
    take(1, finb, landb, outb_ref)


def per_device(npipe, ndev, tokens, routes_f, weight_f, grads, routes_b, weight_b,
               gate_saved, up_saved, gate_proj, up_proj, down_proj):
    half = down_proj.shape[3]
    slots = gate_saved.shape[1]
    rows = ndev * TOK
    nz = ndev // 2
    experts = ndev // min(16, ndev // 2)
    seg = nz // experts
    far = nz // 2
    piece = 512 if half % 512 == 0 else 256

    def flat(value):
        return value[0].reshape(1, TOK)

    kept_gate, kept_up = gate_saved[0].T, up_saved[0].T
    vmem = pl.BlockSpec(memory_space=pltpu.VMEM)
    hbm = pl.BlockSpec(memory_space=pltpu.HBM)
    V = pltpu.VMEM
    dma = pltpu.SemaphoreType.DMA
    outs = pl.pallas_call(
        functools.partial(kernel, ndev, npipe, seg, half, piece),
        out_shape=[jax.ShapeDtypeStruct((TOK, 2 * half), BF16)] * 2,
        in_specs=[hbm] * 2 + [vmem] * 4 + [hbm] * 5,
        out_specs=[vmem] * 2,
        scratch_shapes=[
            V((TOK, 2 * half), BF16),
            V((TOK, 2 * half), BF16),
            V((64, slots), F32),
            V((64, slots), F32),
            V((nz, 16, half + EXT), BF16),
            V((nz, 16, half), BF16),
            V((nz, 16, half), BF16),
            V((nz, 16, half), BF16),
            V((2, far, 16, half), BF16),
            V((2, far, 16, half), BF16),
            V((16, half // 2 + EXT), BF16),
            V((16, half // 2 + EXT), BF16),
            V((16, half // 2), BF16),
            V((16, half // 2), BF16),
            V((16, half), BF16),
            V((nz, 16, 256), BF16),
            V((nz, 16, 256), BF16),
            V((nz, 16, 128), BF16),
            V((nz, 16, 128), BF16),
            V((128, slots), BF16),
            V((128, slots), BF16),
            V((half, 256), BF16),
            V((128, half), BF16),
            V((nz, 16, 256), F32),
            V((nz, 16, 128), F32),
            V((rows, 128), BF16),
            V((rows, 256), BF16),
            V((rows, 128), F32),
            V((rows, 128), F32),
            V((2, 16, half // 2), BF16),
            V((2, 16, half // 2), BF16),
            V((2, 16, half // 2), BF16),
            V((2, 16, half // 2), BF16),
            dma((2, 2, far, SUBS)),
            dma((2, nz, SUBS)),
            dma((2, 2, far, SUBS)),
            dma((2, 2, far, SUBS)),
            dma((3,)),
            dma((3,)),
            dma((2, nz)),
            dma((2, nz)),
            dma((2, 2)),
            dma((2, 2)),
            dma((7,)),
        ],
        compiler_params=pltpu.CompilerParams(
            collective_id=0, has_side_effects=True, vmem_limit_bytes=60 * 1024 * 1024
        ),
    )(
        tokens[0], grads[0], flat(routes_f), flat(weight_f), flat(routes_b), flat(weight_b),
        kept_gate, kept_up, gate_proj[0, 0], up_proj[0, 0], down_proj[0, 0],
    )
    return outs[0][None], outs[1][None]


def solution(mesh):
    row = P("pipe", "expert", None)
    kept = P("pipe", None, "expert")
    weights = P("pipe", "expert", None, None)
    return jax.shard_map(
        functools.partial(per_device, mesh.shape["pipe"], mesh.shape["expert"]), mesh=mesh,
        in_specs=(row, row, row, row, row, row, kept, kept, weights, weights, weights),
        out_specs=(row, row), check_vma=False,
    )
```
